32 devices in a mesh: segment: 4 (over z), blk: 8 (over y, x, core).
Axes of the slice: x: 2, y: 2, z: 4, core: 2. Of those that a mesh axis runs over, the one named last changes fastest.
Arguments:
- layer_inputs: bfloat16 [4, 6, 1024, 256], P('segment', None, 'blk'), may hold values from -6 to 6
- final_cot: bfloat16 [6, 1024, 256], P(None, 'blk'), may hold values from -6 to 6
- attn_weights: bfloat16 [4, 4, 256, 256], P('segment'), may hold values from -0.375 to 0.375
- norm_gain: float32 [4, 256], P('segment'), may hold values from 0.5 to 1.5
- pair_list: int32 [8, 4], replicated, may hold values from 0 to 7, as said below
- pair_count: int32 [8], replicated, may hold values from 2 to 4, as said below
Outputs:
- layer_cots: bfloat16 [4, 6, 1024, 256], P('segment', None, 'blk')
- weight_grads: float32 [4, 4, 256, 256], P('segment')
- gain_grads: float32 [4, 256], P('segment')
The draws below stay inside these ranges and needn't reach their ends.
Inputs may be any that keep to these rules, and one draw needn't show every extreme that they name: `pair_list`: each row holds 4 distinct blocks and its first entry is the row's own block. `pair_count`: some row uses all 4 slots.
All inputs are finite; a program needn't handle non-finite values.
Results may differ from the reference program's by a relative error of at most 0.038.
Values may be sent and summed in bfloat16 or wider, within the bound.
No kernel may reach another device: no remote copies, remote signals or barrier semaphores. Data moves between devices by JAX's collectives and lax.ppermute only.
A program may use at most 64 MiB of HBM per device.

```python
import jax
import jax.numpy as jnp
from jax import lax

D = 256
HEADS = 16
BLK_ATOMS = 128
WALKERS = 6
NBLK = 8
ATOMS = 1024
MAXN = 4
LAYERS = 4


def block_lists(key):
    row_ids = jnp.arange(NBLK, dtype=jnp.int32)
    noise_bits = jax.random.randint(jax.random.fold_in(key, 11), (NBLK, NBLK), 0, 2 ** 20, dtype=jnp.int32)
    ranked = noise_bits * NBLK + row_ids[None, :]
    ranked = jnp.where(row_ids[None, :] == row_ids[:, None], -1, ranked)
    slot_order = jnp.argsort(ranked, axis=1, stable=True)[:, :MAXN].astype(jnp.int32)
    counts = jax.random.randint(jax.random.fold_in(key, 12), (NBLK,), 2, MAXN + 1, dtype=jnp.int32)
    full_row = jax.random.randint(jax.random.fold_in(key, 13), (), 0, NBLK, dtype=jnp.int32)
    counts = jnp.where(row_ids == full_row, MAXN, counts).astype(jnp.int32)
    return (slot_order, counts)


def draw_pair_list(key, part):
    return block_lists(key)[0]


def draw_pair_count(key, part):
    return block_lists(key)[1]


def block_levels(stream_key, dims, split, low, high):
    def one(dim, blocks):
        draws = jax.random.uniform(jax.random.fold_in(jax.random.fold_in(stream_key, 6), dim), (blocks,), jnp.float32, low / len(split), high / len(split))
        return jnp.repeat(jnp.exp(draws), dims[dim] // blocks).reshape((-1,) + (1,) * (len(dims) - dim - 1))

    loudness = one(*split[0])
    for cut in split[1:]:
        loudness = loudness * one(*cut)
    return loudness


def bell_draw(own_key, dims, scale, reach, pieces=(), kind=jnp.bfloat16):
    gain = block_levels(own_key, dims, pieces, -0.22, 0.18) if pieces else 1.0
    entries = jax.random.normal(own_key, dims, jnp.float32) * scale * gain
    return jnp.minimum(jnp.maximum(entries, -reach), reach).astype(kind)


def setup_inputs(seed: int = 0) -> dict:
    key_of = jax.random.split(jax.random.key(seed), 7)
    return {
        "layer_inputs": bell_draw(key_of[0], (LAYERS, WALKERS, ATOMS, D), 1.0, 6.0, ((0, 4), (2, 8))),
        "final_cot": bell_draw(key_of[1], (WALKERS, ATOMS, D), 1.0, 6.0, ((1, 8),)),
        "attn_weights": bell_draw(key_of[2], (LAYERS, 4, D, D), D ** -0.5, 0.375, ((0, 4),)),
        "norm_gain": jnp.clip(1.0 + 0.1 * jax.random.normal(key_of[3], (LAYERS, D), jnp.float32), 0.5, 1.5),
        "pair_list": draw_pair_list(jax.random.fold_in(key_of[6], 71), 0),
        "pair_count": draw_pair_count(jax.random.fold_in(key_of[6], 71), 0),
    }


eps = 1e-05

def rounded(values):
    return lax.optimization_barrier(values.astype(jnp.bfloat16)).astype(jnp.float32)

def rms_parts(inputs, gain_row):
    feats = inputs.astype(jnp.float32)
    inv_rms = lax.rsqrt(lax.optimization_barrier(jnp.mean(feats * feats, axis=-1, keepdims=True)) + eps)
    unit_feat = feats * inv_rms
    normed = (unit_feat * gain_row).astype(jnp.bfloat16)
    return (unit_feat, inv_rms, normed)

def norm_back(normed_grad, unit_feat, inv_rms, gain_row):
    unit_grad = normed_grad * gain_row
    centre = lax.optimization_barrier(jnp.mean(unit_grad * unit_feat, axis=-1, keepdims=True))
    return inv_rms * (unit_grad - unit_feat * centre)

def layer_back(inputs, cotangent, weights, gain_row, pair_list, pair_count):
    block_count = ATOMS // BLK_ATOMS
    head_size = D // HEADS
    score_scale = head_size ** (-0.5)
    unit_feat, inv_rms, normed = rms_parts(inputs, gain_row)
    queries = jnp.dot(normed, weights[0], preferred_element_type=jnp.float32).astype(jnp.bfloat16)
    keys_all = jnp.dot(normed, weights[1], preferred_element_type=jnp.float32).astype(jnp.bfloat16)
    values_all = jnp.dot(normed, weights[2], preferred_element_type=jnp.float32).astype(jnp.bfloat16)
    shape_heads = (block_count, BLK_ATOMS, HEADS, head_size)
    wide_shape = (block_count, MAXN * BLK_ATOMS, HEADS, head_size)
    query_h = queries.reshape(shape_heads).astype(jnp.float32)
    key_h = keys_all.reshape(shape_heads)[pair_list].reshape(wide_shape).astype(jnp.float32)
    value_h = values_all.reshape(shape_heads)[pair_list].reshape(wide_shape).astype(jnp.float32)
    slot_ok = jnp.arange(MAXN)[None, :] < pair_count[:, None]
    column_ok = jnp.repeat(slot_ok, BLK_ATOMS, axis=1)
    scores = jnp.einsum('aqhd,akhd->ahqk', query_h, key_h) * score_scale
    scores = jnp.where(column_ok[:, None, None, :], scores, -1e+30)
    expos = jnp.exp(scores)
    probs = expos / lax.optimization_barrier(jnp.sum(expos, axis=3, keepdims=True))
    probs_b = rounded(probs)
    attended = rounded(jnp.einsum('ahqk,akhd->aqhd', probs_b, value_h))
    out_grad = rounded(jnp.dot(cotangent, weights[3].T, preferred_element_type=jnp.float32)).reshape(shape_heads)
    delta = jnp.moveaxis(lax.optimization_barrier(jnp.sum(out_grad * attended, axis=3)), 2, 1)
    prob_grad = jnp.einsum('aqhd,akhd->ahqk', out_grad, value_h)
    score_grad = rounded(probs * (prob_grad - delta[..., None]) * score_scale)
    query_grad = jnp.einsum('ahqk,akhd->aqhd', score_grad, key_h).reshape(ATOMS, D).astype(jnp.bfloat16)
    part_shape = (block_count, MAXN, BLK_ATOMS, D)
    key_part = rounded(jnp.einsum('ahqk,aqhd->akhd', score_grad, query_h)).reshape(part_shape)
    value_part = rounded(jnp.einsum('ahqk,aqhd->akhd', probs_b, out_grad)).reshape(part_shape)
    zero_blocks = jnp.zeros((block_count, BLK_ATOMS, D), jnp.float32)
    key_grad = zero_blocks.at[pair_list].add(key_part).reshape(ATOMS, D).astype(jnp.bfloat16)
    value_grad = zero_blocks.at[pair_list].add(value_part).reshape(ATOMS, D).astype(jnp.bfloat16)
    normed_grad = jnp.dot(query_grad, weights[0].T, preferred_element_type=jnp.float32) + jnp.dot(key_grad, weights[1].T, preferred_element_type=jnp.float32) + jnp.dot(value_grad, weights[2].T, preferred_element_type=jnp.float32)
    gain_grad = lax.optimization_barrier(jnp.sum(normed_grad * unit_feat, axis=0))
    input_grad = (cotangent.astype(jnp.float32) + norm_back(normed_grad, unit_feat, inv_rms, gain_row)).astype(jnp.bfloat16)
    attended_b = attended.reshape(ATOMS, D).astype(jnp.bfloat16)
    weight_grad = jnp.stack([jnp.dot(normed.T, query_grad, preferred_element_type=jnp.float32), jnp.dot(normed.T, key_grad, preferred_element_type=jnp.float32), jnp.dot(normed.T, value_grad, preferred_element_type=jnp.float32), jnp.dot(attended_b.T, cotangent, preferred_element_type=jnp.float32)])
    return (input_grad, weight_grad, gain_grad)

def reference(layer_inputs, final_cot, attn_weights, norm_gain, pair_list, pair_count):
    cotangent = final_cot
    cot_list = []
    grad_list = []
    gain_list = []
    for layer_no in range(LAYERS - 1, -1, -1):

        def per_walker(walker_pair, layer_no=layer_no):
            return layer_back(walker_pair[0], walker_pair[1], attn_weights[layer_no], norm_gain[layer_no], pair_list, pair_count)
        input_grads, walker_grads, walker_gains = lax.map(per_walker, (layer_inputs[layer_no], cotangent))
        cot_list.insert(0, input_grads)
        grad_list.insert(0, lax.optimization_barrier(jnp.sum(walker_grads, axis=0)))
        gain_list.insert(0, lax.optimization_barrier(jnp.sum(walker_gains, axis=0)))
        cotangent = input_grads
    return (jnp.stack(cot_list), jnp.stack(grad_list), jnp.stack(gain_list))
```

```python
from functools import partial

import jax
import jax.numpy as jnp
from jax import lax
from jax.sharding import PartitionSpec as P

HEADS = 16
EPS = 1e-05
BF = jnp.bfloat16
F32 = jnp.float32


def mm(spec, *args):
    return jnp.einsum(spec, *args, preferred_element_type=F32)


def attend(one, heads, scale):
    q, k, v, out_grad, ok, masks = one
    rows = q.shape[0]
    near = k.shape[0]
    qm = (q[None] * masks).reshape(heads * rows, -1)
    om = (out_grad[None] * masks).reshape(heads * rows, -1)
    scores = mm("xd,kd->xk", qm, k) * scale
    expos = jnp.where(ok[None, :], jnp.exp(scores), 0.0)
    probs = expos / jnp.sum(expos, axis=1, keepdims=True)
    probs_b = probs.astype(BF)
    wide = masks.astype(F32)
    attended = jnp.sum(mm("xk,kd->xd", probs_b, v).reshape(heads, rows, -1) * wide, axis=0)
    attended = attended.astype(BF)
    delta = jnp.sum(
        om.reshape(heads, rows, -1).astype(F32) * attended[None].astype(F32), axis=2
    ).reshape(-1, 1)
    prob_grad = mm("xd,kd->xk", om, v)
    score_grad = (probs * (prob_grad - delta) * scale).astype(BF)
    query_grad = jnp.sum(mm("xk,kd->xd", score_grad, k).reshape(heads, rows, -1) * wide, axis=0)
    key_part = mm("xk,xd->kd", score_grad, qm).astype(BF)
    value_part = mm("xk,xd->kd", probs_b, om).astype(BF)
    return attended, query_grad.astype(BF), key_part, value_part


def per_device(layer_inputs, final_cot, attn_weights, norm_gain, pair_list, pair_count):
    segments = lax.axis_size("segment")
    seg = lax.axis_index("segment")
    blk = lax.axis_index("blk")
    block_count = lax.axis_size("blk")
    walkers, rows, width = layer_inputs.shape[1:]
    slots = pair_list.shape[1]
    head_size = width // HEADS
    half = blk % 2
    chip = blk // 2
    pieces = block_count // 2
    turns = walkers // 2
    own = 2 * rows
    w = attn_weights[0]
    gain = norm_gain

    places = ((pair_list // 2) ^ chip) * 2 + pair_list % 2
    my_lists = lax.dynamic_slice_in_dim(places, 2 * chip, 2, 0)
    my_counts = lax.dynamic_slice_in_dim(pair_count, 2 * chip, 2, 0)
    chosen = (my_lists[:, :, None] == jnp.arange(block_count)).astype(BF)
    ok = jnp.repeat(jnp.arange(slots)[None, :] < my_counts[:, None], rows, axis=1)
    masks = (jnp.arange(width)[None, :] // head_size == jnp.arange(HEADS)[:, None]).astype(BF)
    masks = masks[:, None, :]

    swap = [(i, i ^ 1) for i in range(block_count)]

    def to_walkers(values):
        split = values.reshape(turns, 2, rows, width)
        mine = lax.dynamic_index_in_dim(split, half, 1, keepdims=False)
        other = lax.ppermute(
            lax.dynamic_index_in_dim(split, 1 - half, 1, keepdims=False), "blk", swap
        )
        low = jnp.where(half == 0, mine, other)
        high = jnp.where(half == 0, other, mine)
        return jnp.concatenate([low, high], axis=1)

    x_own = to_walkers(layer_inputs[0])
    last_cot = to_walkers(final_cot)

    def xor_send(value, k):
        return lax.ppermute(value, "blk", [(i, i ^ (2 * k)) for i in range(block_count)])

    def one_walker(x, g):
        feats = x.astype(F32)
        inv = lax.rsqrt(jnp.mean(feats * feats, axis=-1, keepdims=True) + EPS)
        unit = feats * inv
        normed = (unit * gain).astype(BF)
        every = jnp.concatenate(
            [normed] + [xor_send(normed, k) for k in range(1, pieces)], axis=0
        )
        queries = mm("rd,de->re", normed, w[0]).astype(BF).reshape(2, rows, width)
        keys = mm("rd,de->re", every, w[1]).astype(BF).reshape(block_count, rows * width)
        values = mm("rd,de->re", every, w[2]).astype(BF).reshape(block_count, rows * width)
        keys = mm("acb,bx->acx", chosen, keys).astype(BF).reshape(2, slots * rows, width)
        values = mm("acb,bx->acx", chosen, values).astype(BF).reshape(2, slots * rows, width)
        out_grad = mm("rd,ed->re", g, w[3]).astype(BF).reshape(2, rows, width)
        parts = 4 if slots > 4 else 2
        one = partial(attend, heads=HEADS // parts, scale=head_size ** (-0.5))
        args = [jnp.repeat(arg, parts, axis=0) for arg in (queries, keys, values, out_grad, ok)]
        args.append(jnp.concatenate([masks.reshape(parts, HEADS // parts, 1, width)] * 2))
        summed = [
            jnp.sum(part.reshape((2, parts) + part.shape[1:]).astype(F32), axis=1).astype(BF)
            for part in lax.map(one, tuple(args))
        ]
        attended, query_grad, key_part, value_part = summed
        attended = attended.reshape(own, width)
        query_grad = query_grad.reshape(own, width)
        flat = (2, slots, rows * width)
        key_all = mm("acb,acx->bx", chosen, key_part.reshape(flat)).astype(BF)
        value_all = mm("acb,acx->bx", chosen, value_part.reshape(flat)).astype(BF)
        key_all = key_all.reshape(-1, width)
        value_all = value_all.reshape(-1, width)
        normed_grad = mm("re,de->rd", key_all, w[1]) + mm("re,de->rd", value_all, w[2])
        sends = normed_grad.astype(BF)
        total = normed_grad[:own] + mm("re,de->rd", query_grad, w[0])
        for k in range(1, pieces):
            total = total + xor_send(sends[k * own : (k + 1) * own], k).astype(F32)
        unit_grad = total * gain
        centre = jnp.mean(unit_grad * unit, axis=-1, keepdims=True)
        input_grad = (g.astype(F32) + inv * (unit_grad - unit * centre)).astype(BF)
        gain_part = jnp.sum(total * unit, axis=0, keepdims=True)
        grads = jnp.stack(
            [
                mm("rd,re->de", normed, query_grad),
                mm("rd,re->de", every, key_all),
                mm("rd,re->de", every, value_all),
                mm("rd,re->de", attended, g),
            ]
        )
        return input_grad, gain_part, grads

    incoming = jnp.zeros((own, width), BF)
    acc = jnp.zeros((4, width, width), F32)
    gain_acc = jnp.zeros((1, width), F32)
    cots = jnp.zeros((turns, own, width), BF)
    for tick in range(turns + segments - 1):
        turn = tick - (segments - 1 - seg)
        live = (turn >= 0) & (turn < turns)
        turn_at = jnp.clip(turn, 0, turns - 1)
        x = lax.dynamic_index_in_dim(x_own, turn_at, 0, keepdims=False)
        g = jnp.where(seg == segments - 1, last_cot[min(tick, turns - 1)], incoming)
        input_grad, gain_part, grads = one_walker(x, g)
        acc = acc + jnp.where(live, grads, 0.0)
        gain_acc = gain_acc + jnp.where(live, gain_part, 0.0)
        current = lax.dynamic_index_in_dim(cots, turn_at, 0, keepdims=False)
        cots = lax.dynamic_update_index_in_dim(
            cots, jnp.where(live, input_grad, current), turn_at, 0
        )
        if tick < turns + segments - 2:
            incoming = lax.ppermute(
                input_grad, "segment", [(i, (i - 1) % segments) for i in range(segments)]
            )

    halves = cots.reshape(turns, 2, rows, width)
    mine = lax.dynamic_index_in_dim(halves, half, 1, keepdims=False)
    other = lax.ppermute(
        lax.dynamic_index_in_dim(halves, 1 - half, 1, keepdims=False), "blk", swap
    )
    low = jnp.where(half == 0, mine, other)
    high = jnp.where(half == 0, other, mine)
    layer_cots = jnp.stack([low, high], axis=1).reshape(walkers, rows, width)

    flat = acc.astype(BF).reshape(block_count, -1, width)
    extra = jnp.broadcast_to(gain_acc.astype(BF)[None], (block_count, 16, width))
    got = lax.all_to_all(jnp.concatenate([flat, extra], axis=1), "blk", 0, 0)
    total = jnp.sum(got.astype(F32), axis=0)
    grads = lax.all_gather(total[:-16].astype(BF), "blk", axis=0, tiled=True)
    return (
        layer_cots[None],
        grads.astype(F32).reshape(1, 4, width, width),
        total[-16:-15],
    )


def solution(mesh):
    return jax.shard_map(
        per_device,
        mesh=mesh,
        in_specs=(
            P("segment", None, "blk", None),
            P(None, "blk", None),
            P("segment", None, None, None),
            P("segment", None),
            P(),
            P(),
        ),
        out_specs=(
            P("segment", None, "blk", None),
            P("segment", None, None, None),
            P("segment", None),
        ),
        check_vma=False,
    )
```

```python
from functools import partial

import jax
import jax.numpy as jnp
from jax import lax
from jax.sharding import PartitionSpec as P

HEADS = 16
EPS = 1e-05
BF = jnp.bfloat16
F32 = jnp.float32


def mm(spec, *args):
    return jnp.einsum(spec, *args, preferred_element_type=F32)


def attend(one, heads, scale):
    q, k, v, out_grad, ok, masks = one
    rows = q.shape[0]
    near = k.shape[0]
    qm = (q[None] * masks).reshape(heads * rows, -1)
    om = (out_grad[None] * masks).reshape(heads * rows, -1)
    scores = mm("xd,kd->xk", qm, k) * scale
    expos = jnp.where(ok[None, :], jnp.exp(scores), 0.0)
    probs = expos / jnp.sum(expos, axis=1, keepdims=True)
    probs_b = probs.astype(BF)
    wide = masks.astype(F32)
    attended = jnp.sum(mm("xk,kd->xd", probs_b, v).reshape(heads, rows, -1) * wide, axis=0)
    attended = attended.astype(BF)
    delta = jnp.sum(
        om.reshape(heads, rows, -1).astype(F32) * attended[None].astype(F32), axis=2
    ).reshape(-1, 1)
    prob_grad = mm("xd,kd->xk", om, v)
    score_grad = (probs * (prob_grad - delta) * scale).astype(BF)
    query_grad = jnp.sum(mm("xk,kd->xd", score_grad, k).reshape(heads, rows, -1) * wide, axis=0)
    key_part = mm("xk,xd->kd", score_grad, qm).astype(BF)
    value_part = mm("xk,xd->kd", probs_b, om).astype(BF)
    return attended, query_grad.astype(BF), key_part, value_part


def per_device(layer_inputs, final_cot, attn_weights, norm_gain, pair_list, pair_count):
    segments = lax.axis_size("segment")
    seg = lax.axis_index("segment")
    blk = lax.axis_index("blk")
    block_count = lax.axis_size("blk")
    walkers, rows, width = layer_inputs.shape[1:]
    slots = pair_list.shape[1]
    head_size = width // HEADS
    half = blk % 2
    chip = blk // 2
    pieces = block_count // 2
    turns = walkers // 2
    own = 2 * rows
    w = attn_weights[0]
    gain = norm_gain

    places = ((pair_list // 2) ^ chip) * 2 + pair_list % 2
    my_lists = lax.dynamic_slice_in_dim(places, 2 * chip, 2, 0)
    my_counts = lax.dynamic_slice_in_dim(pair_count, 2 * chip, 2, 0)
    chosen = (my_lists[:, :, None] == jnp.arange(block_count)).astype(BF)
    ok = jnp.repeat(jnp.arange(slots)[None, :] < my_counts[:, None], rows, axis=1)
    masks = (jnp.arange(width)[None, :] // head_size == jnp.arange(HEADS)[:, None]).astype(BF)
    masks = masks[:, None, :]

    swap = [(i, i ^ 1) for i in range(block_count)]

    def to_walkers(values):
        split = values.reshape(turns, 2, rows, width)
        mine = lax.dynamic_index_in_dim(split, half, 1, keepdims=False)
        other = lax.ppermute(
            lax.dynamic_index_in_dim(split, 1 - half, 1, keepdims=False), "blk", swap
        )
        low = jnp.where(half == 0, mine, other)
        high = jnp.where(half == 0, other, mine)
        return jnp.concatenate([low, high], axis=1)

    x_own = to_walkers(layer_inputs[0])
    last_cot = to_walkers(final_cot)

    def xor_send(value, k):
        return lax.ppermute(value, "blk", [(i, i ^ (2 * k)) for i in range(block_count)])

    def one_walker(x, g):
        feats = x.astype(F32)
        inv = lax.rsqrt(jnp.mean(feats * feats, axis=-1, keepdims=True) + EPS)
        unit = feats * inv
        normed = (unit * gain).astype(BF)
        every = jnp.concatenate(
            [normed] + [xor_send(normed, k) for k in range(1, pieces)], axis=0
        )
        queries = mm("rd,de->re", normed, w[0]).astype(BF).reshape(2, rows, width)
        keys = mm("rd,de->re", every, w[1]).astype(BF).reshape(block_count, rows * width)
        values = mm("rd,de->re", every, w[2]).astype(BF).reshape(block_count, rows * width)
        keys = mm("acb,bx->acx", chosen, keys).astype(BF).reshape(2, slots * rows, width)
        values = mm("acb,bx->acx", chosen, values).astype(BF).reshape(2, slots * rows, width)
        out_grad = mm("rd,ed->re", g, w[3]).astype(BF).reshape(2, rows, width)
        parts = 4 if slots > 4 else 1
        one = partial(attend, heads=HEADS // parts, scale=head_size ** (-0.5))
        args = [jnp.repeat(arg, parts, axis=0) for arg in (queries, keys, values, out_grad, ok)]
        args.append(jnp.concatenate([masks.reshape(parts, HEADS // parts, 1, width)] * 2))
        summed = [
            jnp.sum(part.reshape((2, parts) + part.shape[1:]).astype(F32), axis=1).astype(BF)
            for part in lax.map(one, tuple(args))
        ]
        attended, query_grad, key_part, value_part = summed
        attended = attended.reshape(own, width)
        query_grad = query_grad.reshape(own, width)
        flat = (2, slots, rows * width)
        key_all = mm("acb,acx->bx", chosen, key_part.reshape(flat)).astype(BF)
        value_all = mm("acb,acx->bx", chosen, value_part.reshape(flat)).astype(BF)
        key_all = key_all.reshape(-1, width)
        value_all = value_all.reshape(-1, width)
        normed_grad = mm("re,de->rd", key_all, w[1]) + mm("re,de->rd", value_all, w[2])
        sends = normed_grad.astype(BF)
        total = normed_grad[:own] + mm("re,de->rd", query_grad, w[0])
        for k in range(1, pieces):
            total = total + xor_send(sends[k * own : (k + 1) * own], k).astype(F32)
        unit_grad = total * gain
        centre = jnp.mean(unit_grad * unit, axis=-1, keepdims=True)
        input_grad = (g.astype(F32) + inv * (unit_grad - unit * centre)).astype(BF)
        gain_part = jnp.sum(total * unit, axis=0, keepdims=True)
        grads = jnp.stack(
            [
                mm("rd,re->de", normed, query_grad),
                mm("rd,re->de", every, key_all),
                mm("rd,re->de", every, value_all),
                mm("rd,re->de", attended, g),
            ]
        )
        return input_grad, gain_part, grads

    incoming = jnp.zeros((own, width), BF)
    acc = jnp.zeros((4, width, width), F32)
    gain_acc = jnp.zeros((1, width), F32)
    cots = jnp.zeros((turns, own, width), BF)
    for tick in range(turns + segments - 1):
        turn = tick - (segments - 1 - seg)
        live = (turn >= 0) & (turn < turns)
        turn_at = jnp.clip(turn, 0, turns - 1)
        x = lax.dynamic_index_in_dim(x_own, turn_at, 0, keepdims=False)
        g = jnp.where(seg == segments - 1, last_cot[min(tick, turns - 1)], incoming)
        input_grad, gain_part, grads = one_walker(x, g)
        acc = acc + jnp.where(live, grads, 0.0)
        gain_acc = gain_acc + jnp.where(live, gain_part, 0.0)
        current = lax.dynamic_index_in_dim(cots, turn_at, 0, keepdims=False)
        cots = lax.dynamic_update_index_in_dim(
            cots, jnp.where(live, input_grad, current), turn_at, 0
        )
        if tick < turns + segments - 2:
            incoming = lax.ppermute(
                input_grad, "segment", [(i, (i - 1) % segments) for i in range(segments)]
            )

    halves = cots.reshape(turns, 2, rows, width)
    mine = lax.dynamic_index_in_dim(halves, half, 1, keepdims=False)
    other = lax.ppermute(
        lax.dynamic_index_in_dim(halves, 1 - half, 1, keepdims=False), "blk", swap
    )
    low = jnp.where(half == 0, mine, other)
    high = jnp.where(half == 0, other, mine)
    layer_cots = jnp.stack([low, high], axis=1).reshape(walkers, rows, width)

    flat = acc.astype(BF).reshape(block_count, -1, width)
    extra = jnp.broadcast_to(gain_acc.astype(BF)[None], (block_count, 16, width))
    got = lax.all_to_all(jnp.concatenate([flat, extra], axis=1), "blk", 0, 0)
    total = jnp.sum(got.astype(F32), axis=0)
    grads = lax.all_gather(total[:-16].astype(BF), "blk", axis=0, tiled=True)
    return (
        layer_cots[None],
        grads.astype(F32).reshape(1, 4, width, width),
        total[-16:-15],
    )


def solution(mesh):
    return jax.shard_map(
        per_device,
        mesh=mesh,
        in_specs=(
            P("segment", None, "blk", None),
            P(None, "blk", None),
            P("segment", None, None, None),
            P("segment", None),
            P(),
            P(),
        ),
        out_specs=(
            P("segment", None, "blk", None),
            P("segment", None, None, None),
            P("segment", None),
        ),
        check_vma=False,
    )
```
